256 devices in a mesh: gx: 16 (over y_hi, x, core), gz: 8 (over z), gy: 2 (over y_lo).
Axes of the slice: x: 4, y: 4 (y_hi: 2, y_lo: 2; y = y_hi * 2 + y_lo), z: 8, core: 2. Of those that a mesh axis runs over, the one named last changes fastest.
Arguments:
- object_slab: float32 [2, 2, 2048, 1024], P(None, 'gy', 'gx', 'gz'), may hold values from -6 to 6
- depth_hops: int32 [16, 2, 1024], P(None, None, 'gz'), may hold values from -256 to 256, as said below
- depth_taps: float32 [16, 2, 8, 1024], P(None, None, None, 'gz'), may hold values from -2 to 2
- column_hops: int32 [16, 2048], P(None, 'gx'), may hold values from -128 to 128, as said below
- column_taps: float32 [16, 8, 2048], P(None, None, 'gx'), may hold values from -2 to 2
- angle_index: int32 [16], replicated, may hold values from 0 to 15, each once
- illumination: float32 [2, 2, 2048], P(None, 'gy', 'gx')
Outputs:
- rotated: float32 [2, 2, 2048, 1024], P(None, 'gy', 'gx', 'gz')
- exit_wave: float32 [2, 2, 2048], P(None, 'gy', 'gx')
The draws below stay inside these ranges and needn't reach their ends.
Inputs may be any that keep to these rules, and one draw needn't show every extreme that they name: `depth_hops`: in every row of every angle, both -256 and 256 occur. `column_hops`: in every angle, both -128 and 128 occur. `angle_index`: each angle occurs once.
All inputs are finite; a program needn't handle non-finite values.
Results may differ from the reference program's by a relative error of at most 0.000028.
Values sent between devices are 32-bit elements; how exact they have to be, the bound alone decides.
No kernel may reach another device: no remote copies, remote signals or barrier semaphores. Data moves between devices by JAX's collectives and lax.ppermute only.
A program may use at most 64 MiB of HBM per device.

```python
import math
import jax
import jax.numpy as jnp

CX = 128
CZ = 128
ANGLES = 16
HOPS_X = 2
HOPS_Z = 1
SLICES = 64
NX = 2048
NZ = 1024
NY = 2


def bounded_hops(key, shape, span):
    first_key, second_key, third_key = jax.random.split(key, 3)
    values = jax.random.randint(first_key, shape, -span, span + 1)
    length = shape[-1]
    lowest = jax.random.randint(second_key, shape[:-1] + (1,), 0, length)
    highest = (lowest + 1 + jax.random.randint(third_key, shape[:-1] + (1,), 0, length - 1)) % length
    places = jnp.arange(length, dtype=jnp.int32)
    values = jnp.where(places == lowest, -span, jnp.where(places == highest, span, values))
    return values.astype(jnp.int32)


def draw_depth_hops(key, part):
    key = jax.random.fold_in(key, 11)
    return bounded_hops(key, (ANGLES, 2, NZ), HOPS_X * CX)


def draw_column_hops(key, part):
    key = jax.random.fold_in(key, 23)
    return bounded_hops(key, (ANGLES, NX), HOPS_Z * CZ)


def draw_illumination(key, part):
    key = jax.random.fold_in(key, 37)
    value_key = jax.random.fold_in(key, 0)
    ramp = 1.0 + 2.0 * jnp.arange(NX, dtype=jnp.float32) / (NX - 1)
    values = jax.random.normal(value_key, (2, NY, NX), jnp.float32)
    return (values * ramp[None, None, :]).astype(jnp.float32)


def level_of(key, extent, cuts, smallest, largest):
    loudness = 1.0
    for dim, blocks in cuts:
        heights = jax.random.uniform(jax.random.fold_in(jax.random.fold_in(key, 6), dim), (blocks,), jnp.float32, smallest / len(cuts), largest / len(cuts))
        loudness = loudness * jnp.repeat(jnp.exp(heights), extent[dim] // blocks).reshape((-1,) + (1,) * (len(extent) - 1 - dim))
    return loudness


def bell_draw(stream_key, extent, deviation, most, pieces=(), held_as=jnp.bfloat16):
    entries = deviation * jax.random.normal(stream_key, extent, jnp.float32)
    if pieces:
        entries = entries * level_of(stream_key, extent, pieces, -0.22, 0.18)
    return jnp.clip(entries, -most, most).astype(held_as)


def setup_inputs(seed: int = 0) -> dict:
    keys = jax.random.split(jax.random.key(seed), 8)
    object_slab = bell_draw(keys[0], (2, NY, NX, NZ), 1.0, 6.0, ((1, 2), (2, 16), (3, 8)), jnp.float32)
    depth_hops = draw_depth_hops(jax.random.fold_in(keys[7], 71), 0)
    depth_taps = bell_draw(keys[2], (ANGLES, 2, 8, NZ), 0.35, 2.0, ((3, 8),), jnp.float32)
    column_hops = draw_column_hops(jax.random.fold_in(keys[7], 71), 0)
    column_taps = bell_draw(keys[4], (ANGLES, 8, NX), 0.35, 2.0, ((2, 16),), jnp.float32)
    angle_index = jax.random.permutation(keys[5], ANGLES).astype(jnp.int32)
    illumination = draw_illumination(jax.random.fold_in(keys[7], 71), 0)
    return dict(object_slab=object_slab, depth_hops=depth_hops, depth_taps=depth_taps, column_hops=column_hops, column_taps=column_taps, angle_index=angle_index, illumination=illumination)


def shear_pass(slab_field, hop_counts, tap_weights):
    length = slab_field.shape[2]
    places = jnp.arange(length, dtype=jnp.int32)[:, None]
    summed = None
    for tap_number in range(8):
        source_rows = (places - hop_counts[None, :].astype(jnp.int32) + (tap_number - 3)) % length
        gathered = jnp.take_along_axis(slab_field, jnp.broadcast_to(source_rows[None, None], slab_field.shape), axis=2)
        term = tap_weights[tap_number][None, None, None, :] * gathered
        summed = term if summed is None else summed + term
    return summed

def reference(object_slab, depth_hops, depth_taps, column_hops, column_taps, angle_index, illumination):
    which = angle_index[0]
    first = shear_pass(object_slab, depth_hops[which, 0], depth_taps[which, 0])
    second = jnp.swapaxes(shear_pass(jnp.swapaxes(first, 2, 3), column_hops[which], column_taps[which]), 2, 3)
    rotated = shear_pass(second, depth_hops[which, 1], depth_taps[which, 1])
    slice_depth = NZ // SLICES
    projected = rotated.reshape(2, NY, NX, SLICES, slice_depth).sum(axis=-1)
    strength = 0.5 / math.sqrt(NZ)
    magnitude = jnp.exp(-strength * projected[1])
    slice_real = magnitude * jnp.cos(strength * projected[0])
    slice_imag = magnitude * jnp.sin(strength * projected[0])
    trans_real = jnp.ones((NY, NX), jnp.float32)
    trans_imag = jnp.zeros((NY, NX), jnp.float32)
    for slice_number in range(SLICES):
        next_real = trans_real * slice_real[:, :, slice_number] - trans_imag * slice_imag[:, :, slice_number]
        next_imag = trans_real * slice_imag[:, :, slice_number] + trans_imag * slice_real[:, :, slice_number]
        trans_real, trans_imag = (next_real, next_imag)
    wave_real = illumination[0] * trans_real - illumination[1] * trans_imag
    wave_imag = illumination[0] * trans_imag + illumination[1] * trans_real
    power = jnp.mean(wave_real * wave_real + wave_imag * wave_imag)
    factor = 1.0 / jnp.sqrt(power + 1e-06)
    exit_wave = jnp.stack([wave_real * factor, wave_imag * factor])
    return (rotated, exit_wave)
```

```python
import functools
import math

import jax
import jax.numpy as jnp
from jax import lax
from jax.experimental import pallas as pl
from jax.experimental.pallas import tpu as pltpu
from jax.sharding import PartitionSpec as P

B = 128
SPAN_X = 256
SPAN_Z = 128
VMEM = pltpu.CompilerParams(vmem_limit_bytes=32 * 1024 * 1024)


def permuted(value, axis, target):
    return lax.ppermute(value, axis, [(i, target(i)) for i in range(lax.axis_size(axis))])


def pairings(count):
    return (
        lambda c: c ^ 1,
        lambda c: (c + 1 if c & 1 else c - 1) % count,
        lambda c: c ^ 2,
        lambda c: (c + 2 if c & 2 else c - 2) % count,
    )


def barrel(ref, kept, top, shifts):
    for bit in range(top, -1, -1):
        step = 1 << bit
        rows = kept if bit == top else -(-(kept + step - 1) // 8) * 8
        moved = (shifts & step) != 0
        for start in range(0, rows, 64):
            size = min(64, rows - start)
            here = ref[pl.ds(start, size), :]
            there = ref[pl.ds(start + step, size), :]
            ref[pl.ds(start, size), :] = jnp.where(moved, there, here)


def tap_sum(ref, first_row, size, taps):
    total = None
    for k in range(8):
        term = taps[k : k + 1, :] * ref[pl.ds(first_row + k, size), :]
        total = term if total is None else total + term
    return total


def assemble(ext, at, size, flag, when_set, when_clear, row_set, row_clear):
    @pl.when(flag == 1)
    def _():
        ext[pl.ds(at, size), :] = when_set[pl.ds(row_set, size), :]

    @pl.when(flag == 0)
    def _():
        ext[pl.ds(at, size), :] = when_clear[pl.ds(row_clear, size), :]


def first_kernel(flags, own, near_a, near_b, far_a, far_b, hops, taps, out, edges, columns, ext, rows):
    odd, second_bit = flags[0], flags[1]
    ext[0:8, :] = jnp.zeros((8, B), jnp.float32)
    ext[792:800, :] = jnp.zeros((8, B), jnp.float32)
    assemble(ext, 8, 8, second_bit, far_a, far_b, 8, 8)
    assemble(ext, 16, 256, odd, near_a, near_b, 0, 0)
    ext[272:528, :] = own[0:256, :]
    assemble(ext, 528, 256, odd, near_b, near_a, 0, 0)
    assemble(ext, 784, 8, second_bit, far_b, far_a, 0, 0)
    barrel(ext, 288, 9, SPAN_X - hops[...])
    weights = taps[...]
    for start in range(0, 256, 64):
        rows[pl.ds(start, 64), :] = tap_sum(ext, start + 13, 64, weights)
    rows[256:264, :] = tap_sum(ext, 269, 8, weights)
    rows[264:272, :] = tap_sum(ext, 5, 8, weights)
    rows[272:384, :] = jnp.zeros((112, B), jnp.float32)
    for tile in range(3):
        turned = rows[pl.ds(tile * B, B), :].T
        out[tile] = turned
        edges[tile, 0:8, :] = turned[0:8, :]
        edges[tile, 8:16, :] = turned[120:128, :]
    columns[0] = own[256:272, :]
    columns[1] = own[272:288, :]
    lane = lax.broadcasted_iota(jnp.int32, (16, B), 1)

    @pl.when(odd == 1)
    def _():
        low = pltpu.roll(near_a[272:288, :], 16, 1)
        columns[2] = jnp.where(lane < 8, near_b[256:272, :], low)

    @pl.when(odd == 0)
    def _():
        low = pltpu.roll(near_b[272:288, :], 16, 1)
        columns[2] = jnp.where(lane < 8, near_a[256:272, :], low)


def second_kernel(flags, own, near_a, near_b, far_a, far_b, columns, out, ext):
    odd, second_bit = flags[2], flags[3]
    for tile in range(3):
        e = ext.at[tile]
        t = tile
        assemble(e, 0, 8, second_bit, far_a.at[t], far_b.at[t], 8, 8)
        assemble(e, 8, 128, odd, near_a.at[t], near_b.at[t], 0, 0)
        e[136:264, :] = own[t]
        assemble(e, 264, 128, odd, near_b.at[t], near_a.at[t], 0, 0)
        assemble(e, 392, 8, second_bit, far_b.at[t], far_a.at[t], 0, 0)
        weights = columns[t]
        barrel(e, 144, 8, SPAN_Z - weights[8:9, :].astype(jnp.int32))
        summed = tap_sum(e, 5, 128, weights).T
        if tile < 2:
            out[pl.ds(tile * B, B), :] = summed
        else:
            out[256:272, :] = summed[0:16, :]


def third_kernel(flags, own, near_a, near_b, hops, taps, keep, send, ext):
    odd, core = flags[0], flags[4]
    ext[0:8, :] = jnp.zeros((8, B), jnp.float32)
    ext[792:800, :] = jnp.zeros((8, B), jnp.float32)
    assemble(ext, 8, 8, odd, near_a, near_b, 264, 264)
    assemble(ext, 16, 256, odd, near_a, near_b, 0, 0)
    ext[272:528, :] = own[0:256, :]
    assemble(ext, 528, 264, odd, near_b, near_a, 0, 0)
    barrel(ext, 288, 9, SPAN_X - hops[...])
    weights = taps[...]
    low = tap_sum(ext, 13, 128, weights)
    high = tap_sum(ext, 13 + 128, 128, weights)
    keep[...] = jnp.where(core == 0, low, high)
    send[...] = jnp.where(core == 0, high, low)


def column_sum_kernel(own, hops, taps, out, ext, moved_ref):
    weights = taps[...]
    ext[0:8, :] = jnp.zeros((8, B), jnp.float32)
    ext[8:264, :] = own[0:256, :]
    ext[264:280, :] = jnp.zeros((16, B), jnp.float32)
    moved_ref[...] = jnp.zeros((640, B), jnp.float32)
    for start in range(0, 264, 88):
        moved_ref[pl.ds(B + start, 88), :] = tap_sum(ext, start + 1, 88, weights)
    shifts = SPAN_X + hops[...]
    for bit in range(7):
        step = 1 << bit
        moved = (shifts & step) != 0
        rows = -(-(264 + 2 * step - 1) // 8) * 8
        for start in reversed(range(0, rows, 64)):
            size = min(64, rows - start)
            here = moved_ref[pl.ds(B + start, size), :]
            there = moved_ref[pl.ds(B + start - step, size), :]
            moved_ref[pl.ds(B + start, size), :] = jnp.where(moved, there, here)
    chosen = lax.broadcasted_iota(jnp.int32, (8, B), 0) == (shifts >> 7)
    sums = lax.dot_general(
        chosen.astype(jnp.float32),
        moved_ref[B:, :],
        (((1,), (1,)), ((), ())),
        precision=lax.Precision.HIGHEST,
        preferred_element_type=jnp.float32,
    )
    out[...] = jnp.zeros((8, B), jnp.float32)
    for block in range(5):
        for tile in range(4):
            if block + tile < 7:
                row = block + tile
                out[row : row + 1, :] += sums[block : block + 1, tile * B : (tile + 1) * B]


def exit_kernel(strength, cells, flags, gathered, illumination, out, acc, loud, proj):
    x_place, y_place = flags[5], flags[6]
    columns = gathered.shape[0] // 2
    row = lax.broadcasted_iota(jnp.int32, (8, B), 0)
    lane = lax.broadcasted_iota(jnp.int32, (columns, B), 1)
    power = None
    for y in range(2):
        for m in range(columns):
            loud[m : m + 1, :] = gathered[2 * m + y, 7:8, :]
        for channel in range(2):
            acc[...] = jnp.zeros(acc.shape, jnp.float32)
            for c in range(columns // 2):
                piece = jnp.where(row < 7, gathered[(2 * c + channel) * 2 + y], 0.0)
                acc[pl.ds(2 * c, 8), :] += piece
            acc[0:8, :] += acc[columns : columns + 8, :]
            acc[columns : columns + 8, :] = acc[0:8, :]
            below = pltpu.roll(acc[2 : columns + 2, :], B - 4, 1)
            above = pltpu.roll(acc[3 : columns + 3, :], B - 4, 1)
            proj[channel, y] = jnp.where(lane < B - 4, below, above)
        root = jnp.exp((-0.5 * strength) * proj[1, y])
        size = 2.0 * ((loud[...] * root) * root)
        part = size * size
        power = part if power is None else power + part
    power = jnp.sum(power, keepdims=True) / cells
    factor = 2.0 / jnp.sqrt(power + 1e-06)
    angle = strength * proj[0, y_place, pl.ds(x_place, 1), :]
    root = jnp.exp((-0.5 * strength) * proj[1, y_place, pl.ds(x_place, 1), :])
    turn_real, turn_imag = jnp.cos(angle), jnp.sin(angle)
    real, imag = 0.5 * illumination[0:1, :], 0.5 * illumination[1:2, :]
    out[0:1, :] = (((real * turn_real - imag * turn_imag) * root) * root) * factor
    out[1:2, :] = (((real * turn_imag + imag * turn_real) * root) * root) * factor


SMEM_SPEC = pl.BlockSpec(memory_space=pltpu.SMEM)
VMEM_SPEC = pl.BlockSpec(memory_space=pltpu.VMEM)


def call(kernel, name, scalars, arrays, outs, scratch):
    f32 = lambda shape: jax.ShapeDtypeStruct(shape, jnp.float32)
    result = pl.pallas_call(
        kernel,
        out_shape=[f32(shape) for shape in outs],
        in_specs=[SMEM_SPEC] * len(scalars) + [VMEM_SPEC] * len(arrays),
        out_specs=[VMEM_SPEC] * len(outs),
        scratch_shapes=[pltpu.VMEM(shape, jnp.float32) for shape in scratch],
        compiler_params=VMEM,
        name=name,
    )(*scalars, *arrays)
    return result[0] if len(outs) == 1 else result


def half_size(illumination):
    real, imag = jnp.abs(illumination[0]), jnp.abs(illumination[1])
    large, small = jnp.maximum(real, imag), jnp.minimum(real, imag)
    ratio = small / jnp.where(large > 0, large, 1.0)
    return (0.5 * large) * jnp.sqrt(1.0 + ratio * ratio)


def everywhere(value, axes, count):
    copies = jnp.broadcast_to(value[None], (count,) + value.shape)
    return lax.all_to_all(copies, axes, 0, 0, tiled=True)


def local(object_slab, depth_hops, depth_taps, column_hops, column_taps, angle_index, illumination):
    which = angle_index[0]
    gx, gz, gy = lax.axis_index("gx"), lax.axis_index("gz"), lax.axis_index("gy")
    size_x, size_z, size_y = lax.axis_size("gx"), lax.axis_size("gz"), lax.axis_size("gy")
    chip, core = gx // 2, gx % 2
    flags = jnp.stack(
        [chip & 1, (chip >> 1) & 1, gz & 1, (gz >> 1) & 1, core, gx, gy, gy]
    ).astype(jnp.int32)
    hops, taps = depth_hops[which], depth_taps[which]
    columns = jnp.concatenate(
        [
            column_taps[which],
            column_hops[which].astype(jnp.float32)[None],
            jnp.zeros((7, B), jnp.float32),
        ]
    )
    slab = object_slab[:, 0]
    mine = jnp.concatenate([jnp.where(core == 0, slab[0], slab[1]), columns])
    theirs = jnp.concatenate([jnp.where(core == 0, slab[1], slab[0]), columns])
    swap = lambda i: i ^ 1
    got = permuted(theirs, "gx", swap)
    low, high = jnp.where(core == 0, mine, got), jnp.where(core == 0, got, mine)
    own = jnp.concatenate([low[:B], high[:B], low[B:], high[B:]])
    ring_x = [
        lambda i, f=f: 2 * f(i // 2) + i % 2 for f in pairings(size_x // 2)
    ]
    ring_z = pairings(size_z)
    edges = jnp.concatenate([own[0:8], own[248:256]])
    received = [permuted(own, "gx", ring_x[0]), permuted(own, "gx", ring_x[1])]
    received += [permuted(edges, "gx", ring_x[2]), permuted(edges, "gx", ring_x[3])]
    first, first_edges, columns = call(
        first_kernel,
        "first_shear",
        [flags],
        [own, *received, hops[0:1], taps[0]],
        [(3, B, B), (3, 16, B), (3, 16, B)],
        [(800, B), (384, B)],
    )
    received = [permuted(first, "gz", ring_z[0]), permuted(first, "gz", ring_z[1])]
    received += [permuted(first_edges, "gz", ring_z[2]), permuted(first_edges, "gz", ring_z[3])]
    second = call(
        second_kernel,
        "second_shear",
        [flags],
        [first, *received, columns],
        [(272, B)],
        [(3, 400, B)],
    )
    received = [permuted(second, "gx", ring_x[0]), permuted(second, "gx", ring_x[1])]
    sums = call(
        column_sum_kernel,
        "depth_sum",
        [],
        [second, hops[1:2], taps[1]],
        [(8, B)],
        [(280, B), (640, B)],
    )
    sums = everywhere(sums, "gz", size_z).sum(axis=0)
    sums = jnp.concatenate([sums[:7], half_size(illumination[:, 0])[None]])
    gathered = everywhere(sums, ("gx", "gy"), size_x * size_y)
    keep, send = call(
        third_kernel,
        "third_shear",
        [flags],
        [second, *received, hops[1:2], taps[1]],
        [(B, B), (B, B)],
        [(800, B)],
    )
    got = permuted(send, "gx", swap)
    rotated = jnp.where(core == 0, jnp.stack([keep, got]), jnp.stack([got, keep]))
    exit_wave = call(
        functools.partial(
            exit_kernel, 0.5 / math.sqrt(B * size_z), float(size_x * B * size_y)
        ),
        "exit_wave",
        [flags],
        [gathered, illumination[:, 0]],
        [(2, B)],
        [(size_x + 8, B), (size_x, B), (2, 2, size_x, B)],
    )
    return (rotated[:, None], exit_wave[:, None])


def solution(mesh):
    return jax.shard_map(
        local,
        mesh=mesh,
        in_specs=(
            P(None, "gy", "gx", "gz"),
            P(None, None, "gz"),
            P(None, None, None, "gz"),
            P(None, "gx"),
            P(None, None, "gx"),
            P(),
            P(None, "gy", "gx"),
        ),
        out_specs=(P(None, "gy", "gx", "gz"), P(None, "gy", "gx")),
        check_vma=False,
    )
```

```python
import functools
import math

import jax
import jax.numpy as jnp
from jax import lax
from jax.experimental import pallas as pl
from jax.experimental.pallas import tpu as pltpu
from jax.sharding import PartitionSpec as P

B = 128
SPAN_X = 256
SPAN_Z = 128
VMEM = pltpu.CompilerParams(vmem_limit_bytes=32 * 1024 * 1024)


def permuted(value, axis, target):
    return lax.ppermute(value, axis, [(i, target(i)) for i in range(lax.axis_size(axis))])


def pairings(count):
    return (
        lambda c: c ^ 1,
        lambda c: (c + 1 if c & 1 else c - 1) % count,
        lambda c: c ^ 2,
        lambda c: (c + 2 if c & 2 else c - 2) % count,
    )


def barrel(ref, kept, top, shifts):
    for bit in range(top, -1, -1):
        step = 1 << bit
        rows = kept if bit == top else -(-(kept + step - 1) // 8) * 8
        moved = (shifts & step) != 0
        for start in range(0, rows, 64):
            size = min(64, rows - start)
            here = ref[pl.ds(start, size), :]
            there = ref[pl.ds(start + step, size), :]
            ref[pl.ds(start, size), :] = jnp.where(moved, there, here)


def tap_sum(ref, first_row, size, taps):
    total = None
    for k in range(8):
        term = taps[k : k + 1, :] * ref[pl.ds(first_row + k, size), :]
        total = term if total is None else total + term
    return total


def assemble(ext, at, size, flag, when_set, when_clear, row_set, row_clear):
    ext[pl.ds(at, size), :] = jnp.where(
        flag == 1, when_set[pl.ds(row_set, size), :], when_clear[pl.ds(row_clear, size), :]
    )


def pushed(ref, at, filled, bits, limit, shifts):
    for bit in range(bits):
        step = 1 << bit
        moved = (shifts & step) != 0
        rows = min(limit, -(-(filled + 2 * step - 1) // 8) * 8)
        for start in reversed(range(0, rows, 64)):
            size = min(64, rows - start)
            here = ref[pl.ds(at + start, size), :]
            there = ref[pl.ds(at + start - step, size), :]
            ref[pl.ds(at + start, size), :] = jnp.where(moved, there, here)


def zero(ref, start, stop):
    ref[start:stop, :] = jnp.zeros((stop - start, B), jnp.float32)


def depth_sum_kernel(cells, params, out, padded, spread):
    weights = params[...]
    zero(padded, 0, 8)
    padded[8:264, :] = cells[0:256, :]
    zero(padded, 264, 280)
    zero(spread, 0, B)
    zero(spread, B + 264, B + 512)
    for start in range(0, 264, 88):
        spread[pl.ds(B + start, 88), :] = tap_sum(padded, start + 1, 88, weights)
    shifts = SPAN_X + weights[8:9, :].astype(jnp.int32)
    pushed(spread, B, 264, 7, 512, shifts)
    row = lax.broadcasted_iota(jnp.int32, (8, B), 0)
    sums = lax.dot_general(
        (row == (shifts >> 7)).astype(jnp.float32),
        spread[B : B + 512, :],
        (((1,), (1,)), ((), ())),
        precision=lax.Precision.HIGHEST,
        preferred_element_type=jnp.float32,
    )
    zero(padded, 0, 8)
    for block in range(5):
        for tile in range(4):
            at = block + tile
            if at < 7:
                piece = sums[block : block + 1, tile * B : (tile + 1) * B]
                padded[at : at + 1, :] += piece
    out[...] = padded[0:8, :]


def pack_kernel(
    flags, mine_own, theirs_own, near_a, near_b, far, mine, theirs
):
    core = flags[4]
    for out, channel, own in ((mine, core, mine_own), (theirs, 1 - core, theirs_own)):
        out[0:128, :] = own[...]
        out[128:256, :] = near_a[channel]
        out[256:384, :] = near_b[channel]
        out[384:392, :] = far[channel]


def first_kernel(flags, mine, got, params, out, edges, ext, rows):
    odd, core = flags[0], flags[4]

    def of_core(number, start, size):
        here, there = mine[pl.ds(start, size), :], got[pl.ds(start, size), :]
        return jnp.where(core == number, here, there)

    below = pl.multiple_of(jnp.where(odd == 1, 128, 256), 128)
    above = pl.multiple_of(jnp.where(odd == 1, 256, 128), 128)
    zero(ext, 0, 8)
    ext[8:16, :] = of_core(0, 384, 8)
    for at, start in ((16, below), (272, 0), (528, above)):
        for number in range(2):
            ext[pl.ds(at + number * B, B), :] = of_core(number, start, B)
    ext[784:792, :] = of_core(1, 384, 8)
    zero(ext, 792, 800)
    weights = params[...]
    barrel(ext, 288, 9, SPAN_X - weights[8:9, :].astype(jnp.int32))
    for start in range(0, 256, 64):
        rows[pl.ds(start, 64), :] = tap_sum(ext, start + 13, 64, weights)
    ends = jnp.concatenate([tap_sum(ext, 269, 8, weights), tap_sum(ext, 5, 8, weights)])
    out[256:272, :] = ends
    edges[32:48, :] = ends
    for tile in range(2):
        turned = rows[pl.ds(tile * B, B), :].T
        out[pl.ds(tile * B, B), :] = turned
        edges[pl.ds(8 * tile, 8), :] = turned[0:8, :]
        edges[pl.ds(16 + 8 * tile, 8), :] = turned[120:128, :]


def second_kernel(
    flags, own, near_a, near_b, far_a, far_b, mine, got, out, ext
):
    odd, second_bit, core = flags[2], flags[3], flags[4]
    of_core = lambda number, rows: jnp.where(core == number, mine[rows, :], got[rows, :])
    columns, beside = slice(0, 16), slice(16, 32)
    lane = lax.broadcasted_iota(jnp.int32, (16, B), 1)
    edge = jnp.where(lane < 8, of_core(1, beside), pltpu.roll(of_core(0, beside), 16, 1))
    tiles = [of_core(0, columns), of_core(1, columns), edge]
    for tile in range(3):
        e = ext.at[tile]
        weights = tiles[tile]
        if tile < 2:
            at, edge = tile * B, 8 * tile
            assemble(e, 0, 8, second_bit, far_a, far_b, 16 + edge, 16 + edge)
            assemble(e, 8, 128, odd, near_a, near_b, at, at)
            e[136:264, :] = own[pl.ds(at, B), :]
            assemble(e, 264, 128, odd, near_b, near_a, at, at)
            assemble(e, 392, 8, second_bit, far_b, far_a, edge, edge)
        else:
            below = jnp.where(odd == 1, near_a[256:272, :], near_b[256:272, :])
            above = jnp.where(odd == 1, near_b[256:272, :], near_a[256:272, :])
            far_below = jnp.where(second_bit == 1, far_a[32:48, :], far_b[32:48, :])
            far_above = jnp.where(second_bit == 1, far_b[32:48, :], far_a[32:48, :])
            e[0:8, 0:16] = far_below.T[120:128, :]
            e[8:136, 0:16] = below.T
            e[136:264, 0:16] = own[256:272, :].T
            e[264:392, 0:16] = above.T
            e[392:400, 0:16] = far_above.T[0:8, :]
        barrel(e, 144, 8, SPAN_Z - weights[8:9, :].astype(jnp.int32))
        summed = tap_sum(e, 5, 128, weights).T
        if tile < 2:
            out[pl.ds(tile * B, B), :] = summed
        else:
            out[256:272, :] = summed[0:16, :]

def third_kernel(flags, own, near_a, near_b, params, keep, send, ext):
    odd, core = flags[0], flags[4]
    zero(ext, 0, 8)
    assemble(ext, 8, 8, odd, near_a, near_b, 264, 264)
    assemble(ext, 16, 256, odd, near_a, near_b, 0, 0)
    ext[272:528, :] = own[0:256, :]
    assemble(ext, 528, 264, odd, near_b, near_a, 0, 0)
    zero(ext, 792, 800)
    weights = params[...]
    barrel(ext, 288, 9, SPAN_X - weights[8:9, :].astype(jnp.int32))
    low = tap_sum(ext, 13, B, weights)
    high = tap_sum(ext, 13 + B, B, weights)
    keep[...] = jnp.where(core == 0, low, high)
    send[...] = jnp.where(core == 0, high, low)


def exit_kernel(strength, cells, flags, gathered, illumination, out, acc, loud, proj):
    x_place, y_place = flags[5], flags[6]
    columns = gathered.shape[0] // 2
    row = lax.broadcasted_iota(jnp.int32, (8, B), 0)
    lane = lax.broadcasted_iota(jnp.int32, (columns, B), 1)
    power = None
    for y in range(2):
        for m in range(columns):
            loud[m : m + 1, :] = gathered[2 * m + y, 7:8, :]
        for channel in range(2):
            acc[...] = jnp.zeros(acc.shape, jnp.float32)
            for c in range(columns // 2):
                piece = jnp.where(row < 7, gathered[(2 * c + channel) * 2 + y], 0.0)
                acc[c % 4, pl.ds(2 * c, 8), :] = piece
            whole = (acc[0] + acc[1]) + (acc[2] + acc[3])
            start = whole[0:8, :] + whole[columns:, :]
            acc[0, 0:columns, :] = whole[0:columns, :]
            acc[0, 0:8, :] = start
            acc[0, columns:, :] = start
            below = pltpu.roll(acc[0, 2 : columns + 2, :], B - 4, 1)
            above = pltpu.roll(acc[0, 3 : columns + 3, :], B - 4, 1)
            proj[channel, y] = jnp.where(lane < B - 4, below, above)
        root = jnp.exp((-0.5 * strength) * proj[1, y])
        size = 2.0 * ((loud[...] * root) * root)
        part = size * size
        power = part if power is None else power + part
    power = jnp.sum(power, keepdims=True) / cells
    factor = 2.0 / jnp.sqrt(power + 1e-06)
    angle = strength * proj[0, y_place, pl.ds(x_place, 1), :]
    root = jnp.exp((-0.5 * strength) * proj[1, y_place, pl.ds(x_place, 1), :])
    turn_real, turn_imag = jnp.cos(angle), jnp.sin(angle)
    real, imag = 0.5 * illumination[0:1, :], 0.5 * illumination[1:2, :]
    out[0:1, :] = (((real * turn_real - imag * turn_imag) * root) * root) * factor
    out[1:2, :] = (((real * turn_imag + imag * turn_real) * root) * root) * factor


SMEM_SPEC = pl.BlockSpec(memory_space=pltpu.SMEM)
VMEM_SPEC = pl.BlockSpec(memory_space=pltpu.VMEM)


def call(kernel, name, scalars, arrays, outs, scratch):
    f32 = lambda shape: jax.ShapeDtypeStruct(shape, jnp.float32)
    result = pl.pallas_call(
        kernel,
        out_shape=[f32(shape) for shape in outs],
        in_specs=[SMEM_SPEC] * len(scalars) + [VMEM_SPEC] * len(arrays),
        out_specs=[VMEM_SPEC] * len(outs),
        scratch_shapes=[pltpu.VMEM(shape, jnp.float32) for shape in scratch],
        compiler_params=VMEM,
        name=name,
    )(*scalars, *arrays)
    return result[0] if len(outs) == 1 else result


def half_size(illumination):
    real, imag = jnp.abs(illumination[0]), jnp.abs(illumination[1])
    large, small = jnp.maximum(real, imag), jnp.minimum(real, imag)
    ratio = small / jnp.where(large > 0, large, 1.0)
    return (0.5 * large) * jnp.sqrt(1.0 + ratio * ratio)


def everywhere(value, axes, count):
    copies = jnp.broadcast_to(value[None], (count,) + value.shape)
    return lax.all_to_all(copies, axes, 0, 0, tiled=True)


def local(object_slab, depth_hops, depth_taps, column_hops, column_taps, angle_index, illumination):
    which = angle_index[0]
    gx, gz, gy = lax.axis_index("gx"), lax.axis_index("gz"), lax.axis_index("gy")
    size_x, size_z, size_y = lax.axis_size("gx"), lax.axis_size("gz"), lax.axis_size("gy")
    chip, core = gx // 2, gx % 2
    flags = jnp.stack(
        [chip & 1, (chip >> 1) & 1, gz & 1, (gz >> 1) & 1, core, gx, gy, gy]
    ).astype(jnp.int32)
    padding = jnp.zeros((7, B), jnp.float32)
    params = lambda taps, hops: jnp.concatenate([taps, hops.astype(jnp.float32)[None], padding])
    columns = params(column_taps[which], column_hops[which])
    ring_x = [lambda i, f=f: 2 * f(i // 2) + i % 2 for f in pairings(size_x // 2)]
    ring_z = pairings(size_z)
    outward = lambda steps: lambda i: ((i ^ 1) + (2 * steps if i & 1 else -2 * steps)) % size_x
    slab = object_slab[:, 0]
    near_b, near_a = permuted(slab, "gx", ring_x[1]), permuted(slab, "gx", ring_x[0])
    far = permuted(jnp.where(core == 0, slab[:, 0:8], slab[:, 120:128]), "gx", outward(2))
    beside = permuted(columns, "gx", outward(1))
    swap = lambda i: i ^ 1
    pair = lambda a, b: [jnp.where(core == 0, a, b), jnp.where(core == 0, b, a)]
    mine, theirs = call(
        pack_kernel,
        "pack",
        [flags],
        [*pair(slab[0], slab[1]), near_a, near_b, far],
        [(392, B), (392, B)],
        [],
    )
    theirs, depth_hops, depth_taps = lax.optimization_barrier((theirs, depth_hops, depth_taps))
    hops, taps = depth_hops[which], depth_taps[which]
    first_params, third_params = params(taps[0], hops[0]), params(taps[1], hops[1])
    got = permuted(theirs, "gx", swap)
    first, edges = call(
        first_kernel,
        "first_shear",
        [flags],
        [mine, got, first_params],
        [(272, B), (48, B)],
        [(800, B), (256, B)],
    )
    columns = jnp.concatenate([columns, beside])
    other_columns = permuted(columns, "gx", swap)
    near_a, near_b = permuted(first, "gz", ring_z[0]), permuted(first, "gz", ring_z[1])
    far_a, far_b = permuted(edges, "gz", ring_z[2]), permuted(edges, "gz", ring_z[3])
    second = call(
        second_kernel,
        "second_shear",
        [flags],
        [first, near_a, near_b, far_a, far_b, columns, other_columns],
        [(272, B)],
        [(3, 400, B)],
    )
    near_a, near_b = permuted(second, "gx", ring_x[0]), permuted(second, "gx", ring_x[1])
    sums = call(
        depth_sum_kernel,
        "depth_sum",
        [],
        [second, third_params],
        [(8, B)],
        [(280, B), (B + 512, B)],
    )
    sums = everywhere(sums, "gz", size_z).sum(axis=0)
    sums = jnp.concatenate([sums[:7], half_size(illumination[:, 0])[None]])
    gathered = everywhere(sums, ("gx", "gy"), size_x * size_y)
    keep, send = call(
        third_kernel,
        "third_shear",
        [flags],
        [second, near_a, near_b, third_params],
        [(B, B), (B, B)],
        [(800, B)],
    )
    rotated = jnp.stack(pair(keep, permuted(send, "gx", swap)))
    exit_wave = call(
        functools.partial(
            exit_kernel, 0.5 / math.sqrt(B * size_z), float(size_x * B * size_y)
        ),
        "exit_wave",
        [flags],
        [gathered, illumination[:, 0]],
        [(2, B)],
        [(4, size_x + 8, B), (size_x, B), (2, 2, size_x, B)],
    )
    return (rotated[:, None], exit_wave[:, None])


def solution(mesh):
    return jax.shard_map(
        local,
        mesh=mesh,
        in_specs=(
            P(None, "gy", "gx", "gz"),
            P(None, None, "gz"),
            P(None, None, None, "gz"),
            P(None, "gx"),
            P(None, None, "gx"),
            P(),
            P(None, "gy", "gx"),
        ),
        out_specs=(P(None, "gy", "gx", "gz"), P(None, "gy", "gx")),
        check_vma=False,
    )
```

```python
import functools
import math

import jax
import jax.numpy as jnp
from jax import lax
from jax.experimental import pallas as pl
from jax.experimental.pallas import tpu as pltpu
from jax.sharding import PartitionSpec as P

B = 128
SPAN_X = 256
SPAN_Z = 128
VMEM = pltpu.CompilerParams(vmem_limit_bytes=32 * 1024 * 1024)


def permuted(value, axis, target):
    return lax.ppermute(value, axis, [(i, target(i)) for i in range(lax.axis_size(axis))])


def pairings(count):
    return (
        lambda c: c ^ 1,
        lambda c: (c + 1 if c & 1 else c - 1) % count,
        lambda c: c ^ 2,
        lambda c: (c + 2 if c & 2 else c - 2) % count,
    )


def barrel(ref, kept, top, shifts):
    for bit in range(top, -1, -1):
        step = 1 << bit
        rows = kept if bit == top else -(-(kept + step - 1) // 8) * 8
        moved = (shifts & step) != 0
        for start in range(0, rows, 64):
            size = min(64, rows - start)
            here = ref[pl.ds(start, size), :]
            there = ref[pl.ds(start + step, size), :]
            ref[pl.ds(start, size), :] = jnp.where(moved, there, here)


def tap_sum(ref, first_row, size, taps):
    total = None
    for k in range(8):
        term = taps[k : k + 1, :] * ref[pl.ds(first_row + k, size), :]
        total = term if total is None else total + term
    return total


def assemble(ext, at, size, flag, when_set, when_clear, row_set, row_clear):
    ext[pl.ds(at, size), :] = jnp.where(
        flag == 1, when_set[pl.ds(row_set, size), :], when_clear[pl.ds(row_clear, size), :]
    )


def pushed(ref, at, filled, bits, limit, shifts):
    for bit in range(bits):
        step = 1 << bit
        moved = (shifts & step) != 0
        rows = min(limit, -(-(filled + 2 * step - 1) // 8) * 8)
        for start in reversed(range(0, rows, 64)):
            size = min(64, rows - start)
            here = ref[pl.ds(at + start, size), :]
            there = ref[pl.ds(at + start - step, size), :]
            ref[pl.ds(at + start, size), :] = jnp.where(moved, there, here)


def zero(ref, start, stop):
    ref[start:stop, :] = jnp.zeros((stop - start, B), jnp.float32)


def depth_sum_kernel(cells, params, out, padded, spread):
    weights = params[...]
    zero(padded, 0, 8)
    padded[8:264, :] = cells[0:256, :]
    zero(padded, 264, 280)
    zero(spread, 0, B)
    zero(spread, B + 264, B + 512)
    for start in range(0, 264, 88):
        spread[pl.ds(B + start, 88), :] = tap_sum(padded, start + 1, 88, weights)
    shifts = SPAN_X + weights[8:9, :].astype(jnp.int32)
    pushed(spread, B, 264, 7, 512, shifts)
    row = lax.broadcasted_iota(jnp.int32, (8, B), 0)
    sums = lax.dot_general(
        (row == (shifts >> 7)).astype(jnp.float32),
        spread[B : B + 512, :],
        (((1,), (1,)), ((), ())),
        precision=lax.Precision.HIGHEST,
        preferred_element_type=jnp.float32,
    )
    zero(padded, 0, 8)
    for block in range(5):
        for tile in range(4):
            at = block + tile
            if at < 7:
                piece = sums[block : block + 1, tile * B : (tile + 1) * B]
                padded[at : at + 1, :] += piece
    out[...] = padded[0:8, :]


def pack_kernel(
    flags, mine_own, theirs_own, below, above, far, mine, theirs
):
    core = flags[4]
    for out, channel, own in ((mine, core, mine_own), (theirs, 1 - core, theirs_own)):
        out[0:128, :] = own[...]
        out[128:256, :] = below[channel]
        out[256:384, :] = above[channel]
        out[384:392, :] = far[channel]


def first_kernel(flags, mine, got, params, out, edges, ext, rows):
    core = flags[4]

    def of_core(number, start, size):
        here, there = mine[pl.ds(start, size), :], got[pl.ds(start, size), :]
        return jnp.where(core == number, here, there)

    zero(ext, 0, 8)
    ext[8:16, :] = of_core(0, 384, 8)
    for at, start in ((16, 128), (272, 0), (528, 256)):
        for number in range(2):
            ext[pl.ds(at + number * B, B), :] = of_core(number, start, B)
    ext[784:792, :] = of_core(1, 384, 8)
    zero(ext, 792, 800)
    weights = params[...]
    barrel(ext, 288, 9, SPAN_X - weights[8:9, :].astype(jnp.int32))
    for start in range(0, 256, 64):
        rows[pl.ds(start, 64), :] = tap_sum(ext, start + 13, 64, weights)
    ends = jnp.concatenate([tap_sum(ext, 269, 8, weights), tap_sum(ext, 5, 8, weights)])
    out[256:272, :] = ends
    edges[32:48, :] = ends
    for tile in range(2):
        turned = rows[pl.ds(tile * B, B), :].T
        out[pl.ds(tile * B, B), :] = turned
        edges[pl.ds(8 * tile, 8), :] = turned[0:8, :]
        edges[pl.ds(16 + 8 * tile, 8), :] = turned[120:128, :]


def second_kernel(
    flags, own, near_a, near_b, far_a, far_b, mine, got, out, ext
):
    odd, second_bit, core = flags[2], flags[3], flags[4]
    of_core = lambda number, rows: jnp.where(core == number, mine[rows, :], got[rows, :])
    columns, beside = slice(0, 16), slice(16, 32)
    lane = lax.broadcasted_iota(jnp.int32, (16, B), 1)
    edge = jnp.where(lane < 8, of_core(1, beside), pltpu.roll(of_core(0, beside), 16, 1))
    tiles = [of_core(0, columns), of_core(1, columns), edge]
    for tile in range(3):
        e = ext.at[tile]
        weights = tiles[tile]
        if tile < 2:
            at, edge = tile * B, 8 * tile
            assemble(e, 0, 8, second_bit, far_a, far_b, 16 + edge, 16 + edge)
            assemble(e, 8, 128, odd, near_a, near_b, at, at)
            e[136:264, :] = own[pl.ds(at, B), :]
            assemble(e, 264, 128, odd, near_b, near_a, at, at)
            assemble(e, 392, 8, second_bit, far_b, far_a, edge, edge)
        else:
            below = jnp.where(odd == 1, near_a[256:272, :], near_b[256:272, :])
            above = jnp.where(odd == 1, near_b[256:272, :], near_a[256:272, :])
            far_below = jnp.where(second_bit == 1, far_a[32:48, :], far_b[32:48, :])
            far_above = jnp.where(second_bit == 1, far_b[32:48, :], far_a[32:48, :])
            e[0:8, 0:16] = far_below.T[120:128, :]
            e[8:136, 0:16] = below.T
            e[136:264, 0:16] = own[256:272, :].T
            e[264:392, 0:16] = above.T
            e[392:400, 0:16] = far_above.T[0:8, :]
        barrel(e, 144, 8, SPAN_Z - weights[8:9, :].astype(jnp.int32))
        summed = tap_sum(e, 5, 128, weights).T
        if tile < 2:
            out[pl.ds(tile * B, B), :] = summed
        else:
            out[256:272, :] = summed[0:16, :]

def third_kernel(flags, own, near_a, near_b, params, keep, send, ext):
    odd, core = flags[0], flags[4]
    zero(ext, 0, 8)
    assemble(ext, 8, 8, odd, near_a, near_b, 264, 264)
    assemble(ext, 16, 256, odd, near_a, near_b, 0, 0)
    ext[272:528, :] = own[0:256, :]
    assemble(ext, 528, 264, odd, near_b, near_a, 0, 0)
    zero(ext, 792, 800)
    weights = params[...]
    barrel(ext, 288, 9, SPAN_X - weights[8:9, :].astype(jnp.int32))
    low = tap_sum(ext, 13, B, weights)
    high = tap_sum(ext, 13 + B, B, weights)
    keep[...] = jnp.where(core == 0, low, high)
    send[...] = jnp.where(core == 0, high, low)


def exit_kernel(strength, cells, flags, gathered, illumination, out, acc, loud, proj):
    x_place, y_place = flags[5], flags[6]
    columns = gathered.shape[0] // 2
    row = lax.broadcasted_iota(jnp.int32, (8, B), 0)
    lane = lax.broadcasted_iota(jnp.int32, (columns, B), 1)
    power = None
    for y in range(2):
        for m in range(columns):
            loud[m : m + 1, :] = gathered[2 * m + y, 7:8, :]
        for channel in range(2):
            acc[...] = jnp.zeros(acc.shape, jnp.float32)
            for c in range(columns // 2):
                piece = jnp.where(row < 7, gathered[(2 * c + channel) * 2 + y], 0.0)
                acc[c % 4, pl.ds(2 * c, 8), :] = piece
            whole = (acc[0] + acc[1]) + (acc[2] + acc[3])
            start = whole[0:8, :] + whole[columns:, :]
            acc[0, 0:columns, :] = whole[0:columns, :]
            acc[0, 0:8, :] = start
            acc[0, columns:, :] = start
            below = pltpu.roll(acc[0, 2 : columns + 2, :], B - 4, 1)
            above = pltpu.roll(acc[0, 3 : columns + 3, :], B - 4, 1)
            proj[channel, y] = jnp.where(lane < B - 4, below, above)
        root = jnp.exp((-0.5 * strength) * proj[1, y])
        size = 2.0 * ((loud[...] * root) * root)
        part = size * size
        power = part if power is None else power + part
    power = jnp.sum(power, keepdims=True) / cells
    factor = 2.0 / jnp.sqrt(power + 1e-06)
    angle = strength * proj[0, y_place, pl.ds(x_place, 1), :]
    root = jnp.exp((-0.5 * strength) * proj[1, y_place, pl.ds(x_place, 1), :])
    turn_real, turn_imag = jnp.cos(angle), jnp.sin(angle)
    real, imag = 0.5 * illumination[0:1, :], 0.5 * illumination[1:2, :]
    out[0:1, :] = (((real * turn_real - imag * turn_imag) * root) * root) * factor
    out[1:2, :] = (((real * turn_imag + imag * turn_real) * root) * root) * factor


SMEM_SPEC = pl.BlockSpec(memory_space=pltpu.SMEM)
VMEM_SPEC = pl.BlockSpec(memory_space=pltpu.VMEM)


def call(kernel, name, scalars, arrays, outs, scratch):
    f32 = lambda shape: jax.ShapeDtypeStruct(shape, jnp.float32)
    result = pl.pallas_call(
        kernel,
        out_shape=[f32(shape) for shape in outs],
        in_specs=[SMEM_SPEC] * len(scalars) + [VMEM_SPEC] * len(arrays),
        out_specs=[VMEM_SPEC] * len(outs),
        scratch_shapes=[pltpu.VMEM(shape, jnp.float32) for shape in scratch],
        compiler_params=VMEM,
        name=name,
    )(*scalars, *arrays)
    return result[0] if len(outs) == 1 else result


def half_size(illumination):
    real, imag = jnp.abs(illumination[0]), jnp.abs(illumination[1])
    large, small = jnp.maximum(real, imag), jnp.minimum(real, imag)
    ratio = small / jnp.where(large > 0, large, 1.0)
    return (0.5 * large) * jnp.sqrt(1.0 + ratio * ratio)


def everywhere(value, axes, count):
    copies = jnp.broadcast_to(value[None], (count,) + value.shape)
    return lax.all_to_all(copies, axes, 0, 0, tiled=True)


def local(object_slab, depth_hops, depth_taps, column_hops, column_taps, angle_index, illumination):
    which = angle_index[0]
    gx, gz, gy = lax.axis_index("gx"), lax.axis_index("gz"), lax.axis_index("gy")
    size_x, size_z, size_y = lax.axis_size("gx"), lax.axis_size("gz"), lax.axis_size("gy")
    chip, core = gx // 2, gx % 2
    flags = jnp.stack(
        [chip & 1, (chip >> 1) & 1, gz & 1, (gz >> 1) & 1, core, gx, gy, gy]
    ).astype(jnp.int32)
    padding = jnp.zeros((7, B), jnp.float32)
    params = lambda taps, hops: jnp.concatenate([taps, hops.astype(jnp.float32)[None], padding])
    columns = params(column_taps[which], column_hops[which])
    ring_x = [lambda i, f=f: 2 * f(i // 2) + i % 2 for f in pairings(size_x // 2)]
    ring_z = pairings(size_z)
    outward = lambda steps: lambda i: ((i ^ 1) + (2 * steps if i & 1 else -2 * steps)) % size_x
    slab = object_slab[:, 0]
    below = permuted(slab, "gx", lambda i: (i + 2) % size_x)
    above = permuted(slab, "gx", lambda i: (i - 2) % size_x)
    far = permuted(jnp.where(core == 0, slab[:, 0:8], slab[:, 120:128]), "gx", outward(2))
    beside = permuted(columns, "gx", outward(1))
    swap = lambda i: i ^ 1
    pair = lambda a, b: [jnp.where(core == 0, a, b), jnp.where(core == 0, b, a)]
    mine, theirs = call(
        pack_kernel,
        "pack",
        [flags],
        [*pair(slab[0], slab[1]), below, above, far],
        [(392, B), (392, B)],
        [],
    )
    hops, taps = depth_hops[which], depth_taps[which]
    first_params, third_params = params(taps[0], hops[0]), params(taps[1], hops[1])
    got = permuted(theirs, "gx", swap)
    first, edges = call(
        first_kernel,
        "first_shear",
        [flags],
        [mine, got, first_params],
        [(272, B), (48, B)],
        [(800, B), (256, B)],
    )
    columns = jnp.concatenate([columns, beside])
    other_columns = permuted(columns, "gx", swap)
    near_a, near_b = permuted(first, "gz", ring_z[0]), permuted(first, "gz", ring_z[1])
    far_a, far_b = permuted(edges, "gz", ring_z[2]), permuted(edges, "gz", ring_z[3])
    second = call(
        second_kernel,
        "second_shear",
        [flags],
        [first, near_a, near_b, far_a, far_b, columns, other_columns],
        [(272, B)],
        [(3, 400, B)],
    )
    near_a, near_b = permuted(second, "gx", ring_x[0]), permuted(second, "gx", ring_x[1])
    sums = call(
        depth_sum_kernel,
        "depth_sum",
        [],
        [second, third_params],
        [(8, B)],
        [(280, B), (B + 512, B)],
    )
    sums = everywhere(sums, "gz", size_z).sum(axis=0)
    sums = jnp.concatenate([sums[:7], half_size(illumination[:, 0])[None]])
    gathered = everywhere(sums, ("gx", "gy"), size_x * size_y)
    keep, send = call(
        third_kernel,
        "third_shear",
        [flags],
        [second, near_a, near_b, third_params],
        [(B, B), (B, B)],
        [(800, B)],
    )
    rotated = jnp.stack(pair(keep, permuted(send, "gx", swap)))
    exit_wave = call(
        functools.partial(
            exit_kernel, 0.5 / math.sqrt(B * size_z), float(size_x * B * size_y)
        ),
        "exit_wave",
        [flags],
        [gathered, illumination[:, 0]],
        [(2, B)],
        [(4, size_x + 8, B), (size_x, B), (2, 2, size_x, B)],
    )
    return (rotated[:, None], exit_wave[:, None])


def solution(mesh):
    return jax.shard_map(
        local,
        mesh=mesh,
        in_specs=(
            P(None, "gy", "gx", "gz"),
            P(None, None, "gz"),
            P(None, None, None, "gz"),
            P(None, "gx"),
            P(None, None, "gx"),
            P(),
            P(None, "gy", "gx"),
        ),
        out_specs=(P(None, "gy", "gx", "gz"), P(None, "gy", "gx")),
        check_vma=False,
    )
```

```python
import functools
import math

import jax
import jax.numpy as jnp
from jax import lax
from jax.experimental import pallas as pl
from jax.experimental.pallas import tpu as pltpu
from jax.sharding import PartitionSpec as P

B = 128
SPAN_X = 256
SPAN_Z = 128
VMEM = pltpu.CompilerParams(vmem_limit_bytes=32 * 1024 * 1024)


def permuted(value, axis, target):
    return lax.ppermute(value, axis, [(i, target(i)) for i in range(lax.axis_size(axis))])


def pairings(count):
    return (
        lambda c: c ^ 1,
        lambda c: (c + 1 if c & 1 else c - 1) % count,
        lambda c: c ^ 2,
        lambda c: (c + 2 if c & 2 else c - 2) % count,
    )


def barrel(ref, kept, top, shifts):
    for bit in range(top, -1, -1):
        step = 1 << bit
        rows = kept if bit == top else -(-(kept + step - 1) // 8) * 8
        moved = (shifts & step) != 0
        for start in range(0, rows, 64):
            size = min(64, rows - start)
            here = ref[pl.ds(start, size), :]
            there = ref[pl.ds(start + step, size), :]
            ref[pl.ds(start, size), :] = jnp.where(moved, there, here)


def tap_sum(ref, first_row, size, taps):
    total = None
    for k in range(8):
        term = taps[k : k + 1, :] * ref[pl.ds(first_row + k, size), :]
        total = term if total is None else total + term
    return total


def assemble(ext, at, size, flag, when_set, when_clear, row_set, row_clear):
    ext[pl.ds(at, size), :] = jnp.where(
        flag == 1, when_set[pl.ds(row_set, size), :], when_clear[pl.ds(row_clear, size), :]
    )


def pushed(ref, at, filled, bits, limit, shifts):
    for bit in range(bits):
        step = 1 << bit
        moved = (shifts & step) != 0
        rows = min(limit, -(-(filled + 2 * step - 1) // 8) * 8)
        for start in reversed(range(0, rows, 64)):
            size = min(64, rows - start)
            here = ref[pl.ds(at + start, size), :]
            there = ref[pl.ds(at + start - step, size), :]
            ref[pl.ds(at + start, size), :] = jnp.where(moved, there, here)


def zero(ref, start, stop):
    ref[start:stop, :] = jnp.zeros((stop - start, B), jnp.float32)


def depth_sum_kernel(cells, params, out, padded, spread):
    weights = params[...]
    zero(padded, 0, 8)
    padded[8:264, :] = cells[0:256, :]
    zero(padded, 264, 280)
    zero(spread, 0, B)
    zero(spread, B + 264, B + 512)
    for start in range(0, 264, 88):
        spread[pl.ds(B + start, 88), :] = tap_sum(padded, start + 1, 88, weights)
    shifts = SPAN_X + weights[8:9, :].astype(jnp.int32)
    pushed(spread, B, 264, 7, 512, shifts)
    row = lax.broadcasted_iota(jnp.int32, (8, B), 0)
    sums = lax.dot_general(
        (row == (shifts >> 7)).astype(jnp.float32),
        spread[B : B + 512, :],
        (((1,), (1,)), ((), ())),
        precision=lax.Precision.HIGHEST,
        preferred_element_type=jnp.float32,
    )
    zero(padded, 0, 8)
    for block in range(5):
        for tile in range(4):
            at = block + tile
            if at < 7:
                piece = sums[block : block + 1, tile * B : (tile + 1) * B]
                padded[at : at + 1, :] += piece
    out[...] = padded[0:8, :]


def pack_kernel(
    flags, mine_own, theirs_own, below, above, far, mine, theirs
):
    core = flags[4]
    for out, channel, own in ((mine, core, mine_own), (theirs, 1 - core, theirs_own)):
        out[0:128, :] = own[...]
        out[128:256, :] = below[channel]
        out[256:384, :] = above[channel]
        out[384:392, :] = far[channel]


def first_kernel(flags, mine, got, params, out, edges, ext, rows):
    core = flags[4]

    def of_core(number, start, size):
        here, there = mine[pl.ds(start, size), :], got[pl.ds(start, size), :]
        return jnp.where(core == number, here, there)

    zero(ext, 0, 8)
    ext[8:16, :] = of_core(0, 384, 8)
    for at, start in ((16, 128), (272, 0), (528, 256)):
        for number in range(2):
            ext[pl.ds(at + number * B, B), :] = of_core(number, start, B)
    ext[784:792, :] = of_core(1, 384, 8)
    zero(ext, 792, 800)
    weights = params[...]
    barrel(ext, 288, 9, SPAN_X - weights[8:9, :].astype(jnp.int32))
    for start in range(0, 256, 64):
        rows[pl.ds(start, 64), :] = tap_sum(ext, start + 13, 64, weights)
    ends = jnp.concatenate([tap_sum(ext, 269, 8, weights), tap_sum(ext, 5, 8, weights)])
    out[256:272, :] = ends
    edges[32:48, :] = ends
    for tile in range(2):
        turned = rows[pl.ds(tile * B, B), :].T
        out[pl.ds(tile * B, B), :] = turned
        edges[pl.ds(8 * tile, 8), :] = turned[0:8, :]
        edges[pl.ds(16 + 8 * tile, 8), :] = turned[120:128, :]


def second_kernel(
    flags, own, near_a, near_b, far_a, far_b, mine, got, out, ext
):
    odd, second_bit, core = flags[2], flags[3], flags[4]
    of_core = lambda number, rows: jnp.where(core == number, mine[rows, :], got[rows, :])
    columns, beside = slice(0, 16), slice(16, 32)
    lane = lax.broadcasted_iota(jnp.int32, (16, B), 1)
    edge = jnp.where(lane < 8, of_core(1, beside), pltpu.roll(of_core(0, beside), 16, 1))
    tiles = [of_core(0, columns), of_core(1, columns), edge]
    for tile in range(3):
        e = ext.at[tile]
        weights = tiles[tile]
        if tile < 2:
            at, edge = tile * B, 8 * tile
            assemble(e, 0, 8, second_bit, far_a, far_b, 16 + edge, 16 + edge)
            assemble(e, 8, 128, odd, near_a, near_b, at, at)
            e[136:264, :] = own[pl.ds(at, B), :]
            assemble(e, 264, 128, odd, near_b, near_a, at, at)
            assemble(e, 392, 8, second_bit, far_b, far_a, edge, edge)
        else:
            below = jnp.where(odd == 1, near_a[256:272, :], near_b[256:272, :])
            above = jnp.where(odd == 1, near_b[256:272, :], near_a[256:272, :])
            far_below = jnp.where(second_bit == 1, far_a[32:48, :], far_b[32:48, :])
            far_above = jnp.where(second_bit == 1, far_b[32:48, :], far_a[32:48, :])
            e[0:8, 0:16] = far_below.T[120:128, :]
            e[8:136, 0:16] = below.T
            e[136:264, 0:16] = own[256:272, :].T
            e[264:392, 0:16] = above.T
            e[392:400, 0:16] = far_above.T[0:8, :]
        barrel(e, 144, 8, SPAN_Z - weights[8:9, :].astype(jnp.int32))
        summed = tap_sum(e, 5, 128, weights).T
        if tile < 2:
            out[pl.ds(tile * B, B), :] = summed
        else:
            out[256:272, :] = summed[0:16, :]

def third_kernel(flags, own, below, above, params, keep, send, ext):
    core = flags[4]
    zero(ext, 0, 8)
    ext[8:16, :] = below[264:272, :]
    ext[16:272, :] = below[0:256, :]
    ext[272:528, :] = own[0:256, :]
    ext[528:792, :] = above[0:264, :]
    zero(ext, 792, 800)
    weights = params[...]
    barrel(ext, 288, 9, SPAN_X - weights[8:9, :].astype(jnp.int32))
    low = tap_sum(ext, 13, B, weights)
    high = tap_sum(ext, 13 + B, B, weights)
    keep[...] = jnp.where(core == 0, low, high)
    send[...] = jnp.where(core == 0, high, low)


def exit_kernel(strength, cells, flags, gathered, illumination, out, acc, loud, proj):
    x_place, y_place = flags[5], flags[6]
    columns = gathered.shape[0] // 2
    row = lax.broadcasted_iota(jnp.int32, (8, B), 0)
    lane = lax.broadcasted_iota(jnp.int32, (columns, B), 1)
    power = None
    for y in range(2):
        for m in range(columns):
            loud[m : m + 1, :] = gathered[2 * m + y, 7:8, :]
        for channel in range(2):
            acc[...] = jnp.zeros(acc.shape, jnp.float32)
            for c in range(columns // 2):
                piece = jnp.where(row < 7, gathered[(2 * c + channel) * 2 + y], 0.0)
                acc[c % 4, pl.ds(2 * c, 8), :] = piece
            whole = (acc[0] + acc[1]) + (acc[2] + acc[3])
            start = whole[0:8, :] + whole[columns:, :]
            acc[0, 0:columns, :] = whole[0:columns, :]
            acc[0, 0:8, :] = start
            acc[0, columns:, :] = start
            below = pltpu.roll(acc[0, 2 : columns + 2, :], B - 4, 1)
            above = pltpu.roll(acc[0, 3 : columns + 3, :], B - 4, 1)
            proj[channel, y] = jnp.where(lane < B - 4, below, above)
        root = jnp.exp((-0.5 * strength) * proj[1, y])
        size = 2.0 * ((loud[...] * root) * root)
        part = size * size
        power = part if power is None else power + part
    power = jnp.sum(power, keepdims=True) / cells
    factor = 2.0 / jnp.sqrt(power + 1e-06)
    angle = strength * proj[0, y_place, pl.ds(x_place, 1), :]
    root = jnp.exp((-0.5 * strength) * proj[1, y_place, pl.ds(x_place, 1), :])
    turn_real, turn_imag = jnp.cos(angle), jnp.sin(angle)
    real, imag = 0.5 * illumination[0:1, :], 0.5 * illumination[1:2, :]
    out[0:1, :] = (((real * turn_real - imag * turn_imag) * root) * root) * factor
    out[1:2, :] = (((real * turn_imag + imag * turn_real) * root) * root) * factor


SMEM_SPEC = pl.BlockSpec(memory_space=pltpu.SMEM)
VMEM_SPEC = pl.BlockSpec(memory_space=pltpu.VMEM)


def call(kernel, name, scalars, arrays, outs, scratch):
    f32 = lambda shape: jax.ShapeDtypeStruct(shape, jnp.float32)
    result = pl.pallas_call(
        kernel,
        out_shape=[f32(shape) for shape in outs],
        in_specs=[SMEM_SPEC] * len(scalars) + [VMEM_SPEC] * len(arrays),
        out_specs=[VMEM_SPEC] * len(outs),
        scratch_shapes=[pltpu.VMEM(shape, jnp.float32) for shape in scratch],
        compiler_params=VMEM,
        name=name,
    )(*scalars, *arrays)
    return result[0] if len(outs) == 1 else result


def half_size(illumination):
    real, imag = jnp.abs(illumination[0]), jnp.abs(illumination[1])
    large, small = jnp.maximum(real, imag), jnp.minimum(real, imag)
    ratio = small / jnp.where(large > 0, large, 1.0)
    return (0.5 * large) * jnp.sqrt(1.0 + ratio * ratio)


def everywhere(value, axes, count):
    copies = jnp.broadcast_to(value[None], (count,) + value.shape)
    return lax.all_to_all(copies, axes, 0, 0, tiled=True)


def local(object_slab, depth_hops, depth_taps, column_hops, column_taps, angle_index, illumination):
    which = angle_index[0]
    gx, gz, gy = lax.axis_index("gx"), lax.axis_index("gz"), lax.axis_index("gy")
    size_x, size_z, size_y = lax.axis_size("gx"), lax.axis_size("gz"), lax.axis_size("gy")
    chip, core = gx // 2, gx % 2
    flags = jnp.stack(
        [chip & 1, (chip >> 1) & 1, gz & 1, (gz >> 1) & 1, core, gx, gy, gy]
    ).astype(jnp.int32)
    padding = jnp.zeros((7, B), jnp.float32)
    params = lambda taps, hops: jnp.concatenate([taps, hops.astype(jnp.float32)[None], padding])
    columns = params(column_taps[which], column_hops[which])
    ring_x = [lambda i, f=f: 2 * f(i // 2) + i % 2 for f in pairings(size_x // 2)]
    ring_z = pairings(size_z)
    outward = lambda steps: lambda i: ((i ^ 1) + (2 * steps if i & 1 else -2 * steps)) % size_x
    slab = object_slab[:, 0]
    below = permuted(slab, "gx", lambda i: (i + 2) % size_x)
    above = permuted(slab, "gx", lambda i: (i - 2) % size_x)
    far = permuted(jnp.where(core == 0, slab[:, 0:8], slab[:, 120:128]), "gx", outward(2))
    beside = permuted(columns, "gx", outward(1))
    swap = lambda i: i ^ 1
    pair = lambda a, b: [jnp.where(core == 0, a, b), jnp.where(core == 0, b, a)]
    mine, theirs = call(
        pack_kernel,
        "pack",
        [flags],
        [*pair(slab[0], slab[1]), below, above, far],
        [(392, B), (392, B)],
        [],
    )
    hops, taps = depth_hops[which], depth_taps[which]
    first_params, third_params = params(taps[0], hops[0]), params(taps[1], hops[1])
    got = permuted(theirs, "gx", swap)
    first, edges = call(
        first_kernel,
        "first_shear",
        [flags],
        [mine, got, first_params],
        [(272, B), (48, B)],
        [(800, B), (256, B)],
    )
    columns = jnp.concatenate([columns, beside])
    other_columns = permuted(columns, "gx", swap)
    near_a, near_b = permuted(first, "gz", ring_z[0]), permuted(first, "gz", ring_z[1])
    far_a, far_b = permuted(edges, "gz", ring_z[2]), permuted(edges, "gz", ring_z[3])
    second = call(
        second_kernel,
        "second_shear",
        [flags],
        [first, near_a, near_b, far_a, far_b, columns, other_columns],
        [(272, B)],
        [(3, 400, B)],
    )
    below = permuted(second, "gx", lambda i: (i + 2) % size_x)
    above = permuted(second, "gx", lambda i: (i - 2) % size_x)
    sums = call(
        depth_sum_kernel,
        "depth_sum",
        [],
        [second, third_params],
        [(8, B)],
        [(280, B), (B + 512, B)],
    )
    sums = everywhere(sums, "gz", size_z).sum(axis=0)
    sums = jnp.concatenate([sums[:7], half_size(illumination[:, 0])[None]])
    gathered = everywhere(sums, ("gx", "gy"), size_x * size_y)
    keep, send = call(
        third_kernel,
        "third_shear",
        [flags],
        [second, below, above, third_params],
        [(B, B), (B, B)],
        [(800, B)],
    )
    rotated = jnp.stack(pair(keep, permuted(send, "gx", swap)))
    exit_wave = call(
        functools.partial(
            exit_kernel, 0.5 / math.sqrt(B * size_z), float(size_x * B * size_y)
        ),
        "exit_wave",
        [flags],
        [gathered, illumination[:, 0]],
        [(2, B)],
        [(4, size_x + 8, B), (size_x, B), (2, 2, size_x, B)],
    )
    return (rotated[:, None], exit_wave[:, None])


def solution(mesh):
    return jax.shard_map(
        local,
        mesh=mesh,
        in_specs=(
            P(None, "gy", "gx", "gz"),
            P(None, None, "gz"),
            P(None, None, None, "gz"),
            P(None, "gx"),
            P(None, None, "gx"),
            P(),
            P(None, "gy", "gx"),
        ),
        out_specs=(P(None, "gy", "gx", "gz"), P(None, "gy", "gx")),
        check_vma=False,
    )
```

```python
import functools
import math

import jax
import jax.numpy as jnp
from jax import lax
from jax.experimental import pallas as pl
from jax.experimental.pallas import tpu as pltpu
from jax.sharding import PartitionSpec as P

B = 128
SPAN_X = 256
SPAN_Z = 128
VMEM = pltpu.CompilerParams(vmem_limit_bytes=32 * 1024 * 1024)


def permuted(value, axis, target):
    return lax.ppermute(value, axis, [(i, target(i)) for i in range(lax.axis_size(axis))])


def pairings(count):
    return (
        lambda c: c ^ 1,
        lambda c: (c + 1 if c & 1 else c - 1) % count,
        lambda c: c ^ 2,
        lambda c: (c + 2 if c & 2 else c - 2) % count,
    )


def barrel(ref, kept, top, shifts):
    for bit in range(top, -1, -1):
        step = 1 << bit
        rows = kept if bit == top else -(-(kept + step - 1) // 8) * 8
        moved = (shifts & step) != 0
        for start in range(0, rows, 64):
            size = min(64, rows - start)
            here = ref[pl.ds(start, size), :]
            there = ref[pl.ds(start + step, size), :]
            ref[pl.ds(start, size), :] = jnp.where(moved, there, here)


def tap_sum(ref, first_row, size, taps):
    total = None
    for k in range(8):
        term = taps[k : k + 1, :] * ref[pl.ds(first_row + k, size), :]
        total = term if total is None else total + term
    return total


def assemble(ext, at, size, flag, when_set, when_clear, row_set, row_clear):
    ext[pl.ds(at, size), :] = jnp.where(
        flag == 1, when_set[pl.ds(row_set, size), :], when_clear[pl.ds(row_clear, size), :]
    )


def pushed(ref, at, filled, bits, limit, shifts):
    for bit in range(bits):
        step = 1 << bit
        moved = (shifts & step) != 0
        rows = min(limit, -(-(filled + 2 * step - 1) // 8) * 8)
        for start in reversed(range(0, rows, 64)):
            size = min(64, rows - start)
            here = ref[pl.ds(at + start, size), :]
            there = ref[pl.ds(at + start - step, size), :]
            ref[pl.ds(at + start, size), :] = jnp.where(moved, there, here)


def zero(ref, start, stop):
    ref[start:stop, :] = jnp.zeros((stop - start, B), jnp.float32)


def depth_sum_kernel(cells, params, out, padded, spread):
    weights = params[...]
    zero(padded, 0, 8)
    padded[8:264, :] = cells[0:256, :]
    zero(padded, 264, 280)
    zero(spread, 0, B)
    zero(spread, B + 264, B + 512)
    for start in range(0, 264, 88):
        spread[pl.ds(B + start, 88), :] = tap_sum(padded, start + 1, 88, weights)
    shifts = SPAN_X + weights[8:9, :].astype(jnp.int32)
    pushed(spread, B, 264, 7, 512, shifts)
    row = lax.broadcasted_iota(jnp.int32, (8, B), 0)
    sums = lax.dot_general(
        (row == (shifts >> 7)).astype(jnp.float32),
        spread[B : B + 512, :],
        (((1,), (1,)), ((), ())),
        precision=lax.Precision.HIGHEST,
        preferred_element_type=jnp.float32,
    )
    zero(padded, 0, 8)
    for block in range(5):
        for tile in range(4):
            at = block + tile
            if at < 7:
                piece = sums[block : block + 1, tile * B : (tile + 1) * B]
                padded[at : at + 1, :] += piece
    out[...] = padded[0:8, :]


def pack_kernel(flags, own, below, above, far, out):
    channel = 1 - flags[4]
    out[0:128, :] = own[...]
    out[128:256, :] = below[channel]
    out[256:384, :] = above[channel]
    out[384:392, :] = far[channel]


def first_kernel(flags, own, below, above, far, got, params, out, edges, ext, rows):
    core = flags[4]

    def of_core(number, start, size):
        if start == 0:
            here = own[...]
        else:
            here = {128: below, 256: above, 384: far}[start][core]
        return jnp.where(core == number, here, got[pl.ds(start, size), :])

    zero(ext, 0, 8)
    ext[8:16, :] = of_core(0, 384, 8)
    for at, start in ((16, 128), (272, 0), (528, 256)):
        for number in range(2):
            ext[pl.ds(at + number * B, B), :] = of_core(number, start, B)
    ext[784:792, :] = of_core(1, 384, 8)
    zero(ext, 792, 800)
    weights = params[...]
    barrel(ext, 288, 9, SPAN_X - weights[8:9, :].astype(jnp.int32))
    for start in range(0, 256, 64):
        rows[pl.ds(start, 64), :] = tap_sum(ext, start + 13, 64, weights)
    ends = jnp.concatenate([tap_sum(ext, 269, 8, weights), tap_sum(ext, 5, 8, weights)])
    out[256:272, :] = ends
    edges[32:48, :] = ends
    for tile in range(2):
        turned = rows[pl.ds(tile * B, B), :].T
        out[pl.ds(tile * B, B), :] = turned
        edges[pl.ds(8 * tile, 8), :] = turned[0:8, :]
        edges[pl.ds(16 + 8 * tile, 8), :] = turned[120:128, :]


def second_kernel(
    flags, own, near_a, near_b, far_a, far_b, mine, got, out, ext
):
    odd, second_bit, core = flags[2], flags[3], flags[4]
    of_core = lambda number, rows: jnp.where(core == number, mine[rows, :], got[rows, :])
    columns, beside = slice(0, 16), slice(16, 32)
    lane = lax.broadcasted_iota(jnp.int32, (16, B), 1)
    edge = jnp.where(lane < 8, of_core(1, beside), pltpu.roll(of_core(0, beside), 16, 1))
    tiles = [of_core(0, columns), of_core(1, columns), edge]
    for tile in range(3):
        e = ext.at[tile]
        weights = tiles[tile]
        if tile < 2:
            at, edge = tile * B, 8 * tile
            assemble(e, 0, 8, second_bit, far_a, far_b, 16 + edge, 16 + edge)
            assemble(e, 8, 128, odd, near_a, near_b, at, at)
            e[136:264, :] = own[pl.ds(at, B), :]
            assemble(e, 264, 128, odd, near_b, near_a, at, at)
            assemble(e, 392, 8, second_bit, far_b, far_a, edge, edge)
        else:
            below = jnp.where(odd == 1, near_a[256:272, :], near_b[256:272, :])
            above = jnp.where(odd == 1, near_b[256:272, :], near_a[256:272, :])
            far_below = jnp.where(second_bit == 1, far_a[32:48, :], far_b[32:48, :])
            far_above = jnp.where(second_bit == 1, far_b[32:48, :], far_a[32:48, :])
            e[0:8, 0:16] = far_below.T[120:128, :]
            e[8:136, 0:16] = below.T
            e[136:264, 0:16] = own[256:272, :].T
            e[264:392, 0:16] = above.T
            e[392:400, 0:16] = far_above.T[0:8, :]
        barrel(e, 144, 8, SPAN_Z - weights[8:9, :].astype(jnp.int32))
        summed = tap_sum(e, 5, 128, weights).T
        if tile < 2:
            out[pl.ds(tile * B, B), :] = summed
        else:
            out[256:272, :] = summed[0:16, :]

def third_kernel(flags, own, near_a, near_b, params, keep, send, ext):
    odd, core = flags[0], flags[4]
    zero(ext, 0, 8)
    assemble(ext, 8, 8, odd, near_a, near_b, 264, 264)
    assemble(ext, 16, 256, odd, near_a, near_b, 0, 0)
    ext[272:528, :] = own[0:256, :]
    assemble(ext, 528, 264, odd, near_b, near_a, 0, 0)
    zero(ext, 792, 800)
    weights = params[...]
    barrel(ext, 288, 9, SPAN_X - weights[8:9, :].astype(jnp.int32))
    low = tap_sum(ext, 13, B, weights)
    high = tap_sum(ext, 13 + B, B, weights)
    keep[...] = jnp.where(core == 0, low, high)
    send[...] = jnp.where(core == 0, high, low)


def exit_kernel(strength, cells, flags, gathered, illumination, out, acc, loud, proj):
    x_place, y_place = flags[5], flags[6]
    columns = gathered.shape[0] // 2
    row = lax.broadcasted_iota(jnp.int32, (8, B), 0)
    lane = lax.broadcasted_iota(jnp.int32, (columns, B), 1)
    power = None
    for y in range(2):
        for m in range(columns):
            loud[m : m + 1, :] = gathered[2 * m + y, 7:8, :]
        for channel in range(2):
            acc[...] = jnp.zeros(acc.shape, jnp.float32)
            for c in range(columns // 2):
                piece = jnp.where(row < 7, gathered[(2 * c + channel) * 2 + y], 0.0)
                acc[c % 4, pl.ds(2 * c, 8), :] = piece
            whole = (acc[0] + acc[1]) + (acc[2] + acc[3])
            start = whole[0:8, :] + whole[columns:, :]
            acc[0, 0:columns, :] = whole[0:columns, :]
            acc[0, 0:8, :] = start
            acc[0, columns:, :] = start
            below = pltpu.roll(acc[0, 2 : columns + 2, :], B - 4, 1)
            above = pltpu.roll(acc[0, 3 : columns + 3, :], B - 4, 1)
            proj[channel, y] = jnp.where(lane < B - 4, below, above)
        root = jnp.exp((-0.5 * strength) * proj[1, y])
        size = 2.0 * ((loud[...] * root) * root)
        part = size * size
        power = part if power is None else power + part
    power = jnp.sum(power, keepdims=True) / cells
    factor = 2.0 / jnp.sqrt(power + 1e-06)
    angle = strength * proj[0, y_place, pl.ds(x_place, 1), :]
    root = jnp.exp((-0.5 * strength) * proj[1, y_place, pl.ds(x_place, 1), :])
    turn_real, turn_imag = jnp.cos(angle), jnp.sin(angle)
    real, imag = 0.5 * illumination[0:1, :], 0.5 * illumination[1:2, :]
    out[0:1, :] = (((real * turn_real - imag * turn_imag) * root) * root) * factor
    out[1:2, :] = (((real * turn_imag + imag * turn_real) * root) * root) * factor


SMEM_SPEC = pl.BlockSpec(memory_space=pltpu.SMEM)
VMEM_SPEC = pl.BlockSpec(memory_space=pltpu.VMEM)


def call(kernel, name, scalars, arrays, outs, scratch):
    f32 = lambda shape: jax.ShapeDtypeStruct(shape, jnp.float32)
    result = pl.pallas_call(
        kernel,
        out_shape=[f32(shape) for shape in outs],
        in_specs=[SMEM_SPEC] * len(scalars) + [VMEM_SPEC] * len(arrays),
        out_specs=[VMEM_SPEC] * len(outs),
        scratch_shapes=[pltpu.VMEM(shape, jnp.float32) for shape in scratch],
        compiler_params=VMEM,
        name=name,
    )(*scalars, *arrays)
    return result[0] if len(outs) == 1 else result


def half_size(illumination):
    real, imag = jnp.abs(illumination[0]), jnp.abs(illumination[1])
    large, small = jnp.maximum(real, imag), jnp.minimum(real, imag)
    ratio = small / jnp.where(large > 0, large, 1.0)
    return (0.5 * large) * jnp.sqrt(1.0 + ratio * ratio)


def everywhere(value, axes, count):
    copies = jnp.broadcast_to(value[None], (count,) + value.shape)
    return lax.all_to_all(copies, axes, 0, 0, tiled=True)


def local(object_slab, depth_hops, depth_taps, column_hops, column_taps, angle_index, illumination):
    which = angle_index[0]
    gx, gz, gy = lax.axis_index("gx"), lax.axis_index("gz"), lax.axis_index("gy")
    size_x, size_z, size_y = lax.axis_size("gx"), lax.axis_size("gz"), lax.axis_size("gy")
    chip, core = gx // 2, gx % 2
    flags = jnp.stack(
        [chip & 1, (chip >> 1) & 1, gz & 1, (gz >> 1) & 1, core, gx, gy, gy]
    ).astype(jnp.int32)
    padding = jnp.zeros((7, B), jnp.float32)
    params = lambda taps, hops: jnp.concatenate([taps, hops.astype(jnp.float32)[None], padding])
    columns = params(column_taps[which], column_hops[which])
    ring_x = [lambda i, f=f: 2 * f(i // 2) + i % 2 for f in pairings(size_x // 2)]
    ring_z = pairings(size_z)
    outward = lambda steps: lambda i: ((i ^ 1) + (2 * steps if i & 1 else -2 * steps)) % size_x
    slab = object_slab[:, 0]
    below = permuted(slab, "gx", lambda i: (i + 2) % size_x)
    above = permuted(slab, "gx", lambda i: (i - 2) % size_x)
    far = permuted(jnp.where(core == 0, slab[:, 0:8], slab[:, 120:128]), "gx", outward(2))
    beside = permuted(columns, "gx", outward(1))
    swap = lambda i: i ^ 1
    pair = lambda a, b: [jnp.where(core == 0, a, b), jnp.where(core == 0, b, a)]
    mine, theirs = pair(slab[0], slab[1])
    theirs = call(
        pack_kernel, "pack", [flags], [theirs, below, above, far], [(392, B)], []
    )
    hops, taps = depth_hops[which], depth_taps[which]
    first_params, third_params = params(taps[0], hops[0]), params(taps[1], hops[1])
    got = permuted(theirs, "gx", swap)
    first, edges = call(
        first_kernel,
        "first_shear",
        [flags],
        [mine, below, above, far, got, first_params],
        [(272, B), (48, B)],
        [(800, B), (256, B)],
    )
    columns = jnp.concatenate([columns, beside])
    other_columns = permuted(columns, "gx", swap)
    near_a, near_b = permuted(first, "gz", ring_z[0]), permuted(first, "gz", ring_z[1])
    far_a, far_b = permuted(edges, "gz", ring_z[2]), permuted(edges, "gz", ring_z[3])
    second = call(
        second_kernel,
        "second_shear",
        [flags],
        [first, near_a, near_b, far_a, far_b, columns, other_columns],
        [(272, B)],
        [(3, 400, B)],
    )
    near_a, near_b = permuted(second, "gx", ring_x[0]), permuted(second, "gx", ring_x[1])
    sums = call(
        depth_sum_kernel,
        "depth_sum",
        [],
        [second, third_params],
        [(8, B)],
        [(280, B), (B + 512, B)],
    )
    sums = everywhere(sums, "gz", size_z).sum(axis=0)
    sums = jnp.concatenate([sums[:7], half_size(illumination[:, 0])[None]])
    gathered = everywhere(sums, ("gx", "gy"), size_x * size_y)
    keep, send = call(
        third_kernel,
        "third_shear",
        [flags],
        [second, near_a, near_b, third_params],
        [(B, B), (B, B)],
        [(800, B)],
    )
    rotated = jnp.stack(pair(keep, permuted(send, "gx", swap)))
    exit_wave = call(
        functools.partial(
            exit_kernel, 0.5 / math.sqrt(B * size_z), float(size_x * B * size_y)
        ),
        "exit_wave",
        [flags],
        [gathered, illumination[:, 0]],
        [(2, B)],
        [(4, size_x + 8, B), (size_x, B), (2, 2, size_x, B)],
    )
    return (rotated[:, None], exit_wave[:, None])


def solution(mesh):
    return jax.shard_map(
        local,
        mesh=mesh,
        in_specs=(
            P(None, "gy", "gx", "gz"),
            P(None, None, "gz"),
            P(None, None, None, "gz"),
            P(None, "gx"),
            P(None, None, "gx"),
            P(),
            P(None, "gy", "gx"),
        ),
        out_specs=(P(None, "gy", "gx", "gz"), P(None, "gy", "gx")),
        check_vma=False,
    )
```
